512 devices in a mesh: design: 16 (over y, x_lo, core), seq: 32 (over x_hi, z).
Axes of the slice: x: 4 (x_hi: 2, x_lo: 2; x = x_hi * 2 + x_lo), y: 4, z: 16, core: 2. Of those that a mesh axis runs over, the one named last changes fastest.
Arguments:
- window_x: bfloat16 [16, 512, 8192], P('design', 'seq'), may hold values from -6 to 6
- norm_gain: float32 [8192], replicated, may hold values from 0.5 to 1.5
- proj_weight: bfloat16 [8192, 3, 4096], P('design', None, 'seq'), may hold values from -0.0625 to 0.0625
- proj_tail: bfloat16 [16, 6, 3, 4096], P('design', None, None, 'seq'), may hold values from -6 to 6
- short_taps: float32 [7, 3, 4096], P(None, None, 'seq'), may hold values from -2 to 2
- decay_rates: float32 [4096, 16], replicated, may hold values from 8.680556e-06 to 0.035
- residues: float32 [4096, 16], P('seq'), may hold values from 0 to 0.03
- skip_bias: float32 [4096], P('seq'), may hold values from -6 to 6
- context_u: bfloat16 [16, 4096, 4096], P('design', 'seq'), may hold values from -6 to 6
- context_tokens: int32 [16, 4096], P('design', 'seq'), may hold values from 0 to 4, as said below
Outputs:
- mixed: bfloat16 [16, 512, 4096], P('design', None, 'seq')
The draws below stay inside these ranges and needn't reach their ends.
Inputs may be any that keep to these rules, and one draw needn't show every extreme that they name: `context_tokens`: 0 marks padding and fills a prefix of 1 to 65 positions of each design's context; 1 to 4 are bases.
All inputs are finite; a program needn't handle non-finite values.
Results may differ from the reference program's by a relative error of at most 0.0059.
The reference program's roundings to bfloat16 on the way (of `normed` and `features`) count: a program that leaves them out, or rounds other values in their place, can miss the bound.
Values may be sent and summed in bfloat16 or wider, within the bound.
No kernel may reach another device: no remote copies, remote signals or barrier semaphores. Data moves between devices by JAX's collectives and lax.ppermute only.
A program may use at most 128 MiB of HBM per device.

```python
import math
import jax
import jax.numpy as jnp
from jax import lax

D = 8192
CH = 4096
MODES = 16
SHORT = 7
CTX_DEV = 128
DESIGNS = 16
WIN = 512
CTX = 4096


def mode_table(key, band_share, slow_share):
    class_key, level_key = jax.random.split(key)
    chain = CTX + WIN
    classes = jax.random.randint(class_key, (CH, MODES), 0, 100)
    level = jax.random.uniform(level_key, (CH, MODES), jnp.float32)
    slow_rates = jnp.exp(math.log(0.04 / chain) + level * math.log(25.0))
    band_rates = jnp.exp(math.log(0.0015) + level * math.log(0.008 / 0.0015))
    fast_rates = jnp.exp(math.log(0.02) + level * math.log(1.75))
    rates = jnp.where(classes < band_share, band_rates, jnp.where(classes < band_share + slow_share, slow_rates, fast_rates))
    return rates


def draw_decay_rates(key, part):
    rates = mode_table(key, 65, 20)
    return rates.astype(jnp.float32)


def draw_residues(key, part):
    rates = mode_table(key, 65, 20)
    key = jax.random.fold_in(key, 41)
    gains = jax.random.uniform(key, (CH, MODES), jnp.float32, 0.4, 1.6)
    floor_rate = 1.0 / (CTX + WIN)
    values = 0.07 * gains * jnp.sqrt(jnp.maximum(rates, floor_rate))
    return values.astype(jnp.float32)


def draw_context_u(key, part):
    key = jax.random.fold_in(key, 29)
    noise_key, period_key, phase_key, pair_key = jax.random.split(key, 4)
    positions = jnp.arange(CTX, dtype=jnp.int32).astype(jnp.float32)
    periods = jnp.exp(math.log(96.0) + jax.random.uniform(period_key, (CH,), jnp.float32) * math.log(320.0 / 96.0))
    phases = jax.random.uniform(phase_key, (DESIGNS, 1, CH), jnp.float32, -math.pi, math.pi)
    pattern = 0.8 * jnp.cos(2.0 * math.pi * positions[None, :, None] / periods[None, None, :] + phases)
    shard_count = CTX // CTX_DEV
    block_width = CH // shard_count
    pairing = jax.random.permutation(pair_key, shard_count)
    shard_of = jnp.arange(CTX, dtype=jnp.int32) // CTX_DEV
    block_of = jnp.arange(CH, dtype=jnp.int32) // block_width
    boost = jnp.where(pairing[shard_of][:, None] == block_of[None, :], 1.5, 1.0).astype(jnp.float32)
    noise = jax.random.truncated_normal(noise_key, -3.4, 3.4, (DESIGNS, CTX, CH), jnp.float32)
    values = noise * boost[None] + pattern
    return values.astype(jnp.bfloat16)


def draw_context_tokens(key, part):
    start_key, base_key, chosen_key = jax.random.split(jax.random.fold_in(key, 17), 3)
    longest = CTX // 64 + 1
    pad_length = jax.random.randint(start_key, (DESIGNS, 1), 1, longest + 1)
    chosen = jax.random.randint(chosen_key, (), 0, DESIGNS)
    design_ids = jnp.arange(DESIGNS, dtype=jnp.int32)[:, None]
    pad_length = jnp.where(design_ids == chosen, longest, pad_length)
    bases = jax.random.randint(base_key, (DESIGNS, CTX), 1, 5)
    places = jnp.arange(CTX, dtype=jnp.int32)[None, :]
    return jnp.where(places < pad_length, 0, bases).astype(jnp.int32)


def steps_of(stream_key, shape, pieces, least, high):
    def one(dim, parts):
        draws = jax.random.uniform(jax.random.fold_in(jax.random.fold_in(stream_key, 6), dim), (parts,), jnp.float32, least / len(pieces), high / len(pieces))
        return jnp.repeat(jnp.exp(draws), shape[dim] // parts).reshape((-1,) + (1,) * (len(shape) - dim - 1))

    factor_of = one(*pieces[0])
    for cut in pieces[1:]:
        factor_of = factor_of * one(*cut)
    return factor_of


def gaussian(key, shape, scale, most, pieces=(), held_as=jnp.bfloat16):
    result = scale * jax.random.normal(key, shape, jnp.float32)
    if pieces:
        result = result * steps_of(key, shape, pieces, -0.22, 0.18)
    return jnp.clip(result, -most, most).astype(held_as)


def setup_inputs(seed: int = 0) -> dict:
    key_list = jax.random.split(jax.random.key(seed), 11)
    return {
        "window_x": gaussian(key_list[0], (DESIGNS, WIN, D), 1.0, 6.0, ((0, 16), (1, 32))),
        "norm_gain": jnp.clip(1.0 + 0.1 * jax.random.normal(key_list[1], (D,), jnp.float32), 0.5, 1.5),
        "proj_weight": gaussian(key_list[2], (D, 3, CH), D ** -0.5, 0.0625, ((0, 16), (2, 32))),
        "proj_tail": gaussian(key_list[3], (DESIGNS, SHORT - 1, 3, CH), 1.0, 6.0, ((0, 16), (3, 32))),
        "short_taps": gaussian(key_list[4], (SHORT, 3, CH), SHORT ** -0.5, 2.0, ((2, 32),), jnp.float32),
        "decay_rates": draw_decay_rates(jax.random.fold_in(key_list[10], 71), 0),
        "residues": draw_residues(jax.random.fold_in(key_list[10], 71), 0),
        "skip_bias": gaussian(key_list[7], (CH,), 0.5, 6.0, ((0, 32),), jnp.float32),
        "context_u": draw_context_u(jax.random.fold_in(key_list[10], 71), 0),
        "context_tokens": draw_context_tokens(jax.random.fold_in(key_list[10], 71), 0),
    }


def reference(window_x, norm_gain, proj_weight, proj_tail, short_taps, decay_rates, residues, skip_bias, context_u, context_tokens):
    window = window_x.shape[1]
    history = context_u.shape[1]
    width = window_x.shape[2]
    channels = proj_weight.shape[2]
    full_length = history + window
    weights_flat = proj_weight.reshape(width, 3 * channels)
    offsets = jnp.arange(full_length).astype(jnp.float32)
    kernel = jnp.zeros((full_length, channels), jnp.float32)
    for mode_index in range(MODES):
        kernel = kernel + residues[:, mode_index][None, :] * jnp.exp(-decay_rates[:, mode_index][None, :] * offsets[:, None])
    length_fft = 2 * full_length
    kernel_spec = jnp.fft.rfft(kernel, n=length_fft, axis=0)

    def one_design(design_items):
        design_rows, tail_rows, history_u, tokens = design_items
        rows_f = design_rows.astype(jnp.float32)
        meansq = lax.optimization_barrier(jnp.mean(rows_f * rows_f, axis=-1, keepdims=True))
        normed = (rows_f * lax.rsqrt(meansq + 1e-06) * norm_gain[None, :]).astype(jnp.bfloat16)
        features = jnp.dot(normed, weights_flat, preferred_element_type=jnp.float32).astype(jnp.bfloat16)
        features = features.reshape(window, 3, channels)
        extended = jnp.concatenate([tail_rows, features], axis=0).astype(jnp.float32)
        filtered = jnp.zeros((window, 3, channels), jnp.float32)
        for tap_index in range(SHORT):
            begin_row = SHORT - 1 - tap_index
            filtered = filtered + short_taps[tap_index][None] * extended[begin_row:begin_row + window]
        inner_term = filtered[:, 1] * filtered[:, 2]
        masked = jnp.where((tokens != 0)[:, None], history_u.astype(jnp.float32), jnp.zeros((), jnp.float32))
        joined = jnp.concatenate([masked, inner_term], axis=0)
        spectrum = jnp.fft.rfft(joined, n=length_fft, axis=0) * kernel_spec
        longconv = jnp.fft.irfft(spectrum, n=length_fft, axis=0)[history:full_length]
        return (filtered[:, 0] * (longconv + skip_bias[None, :] * inner_term)).astype(jnp.bfloat16)
    return lax.map(one_design, (window_x, proj_tail, context_u, context_tokens))
```

```python
import functools

import jax
import jax.numpy as jnp
from jax import lax
from jax.experimental import pallas as pl
from jax.experimental.pallas import tpu as pltpu
from jax.sharding import Mesh
from jax.sharding import PartitionSpec as P

F32 = jnp.float32
BF16 = jnp.bfloat16
HALO = 8


def step(axis, size, by):
    return functools.partial(
        lax.ppermute, axis_name=axis, perm=[(i, (i + by) % size) for i in range(size)]
    )


def norm_kernel(blocks, x_ref, gain_ref, order_ref, keep_ref, give_ref):
    rows, width = x_ref.shape
    depth = width // blocks
    half = blocks // 2
    total = jnp.zeros((rows, depth), F32)
    for b in range(blocks):
        part = x_ref[:, b * depth : (b + 1) * depth].astype(F32)
        total = total + part * part
    scale = lax.rsqrt(jnp.sum(total, axis=1, keepdims=True) / width + 1e-6)
    for b in range(blocks):
        source = pl.multiple_of(order_ref[b] * depth, depth)
        part = x_ref[:, pl.ds(source, depth)].astype(F32)
        value = (part * scale * gain_ref[:, pl.ds(source, depth)]).astype(BF16)
        out_ref = keep_ref if b < half else give_ref
        place = (b % half) * depth
        out_ref[:, place : place + depth] = value


def norm(x, gain, order):
    rows, width = x.shape
    blocks = order.shape[0]
    shape = jax.ShapeDtypeStruct((rows, width // 2), BF16)
    vmem = pl.BlockSpec(memory_space=pltpu.VMEM)
    return pl.pallas_call(
        functools.partial(norm_kernel, blocks),
        out_shape=(shape, shape),
        in_specs=[vmem, vmem, pl.BlockSpec(memory_space=pltpu.SMEM)],
        out_specs=(vmem, vmem),
        compiler_params=pltpu.CompilerParams(vmem_limit_bytes=16 << 20),
        cost_estimate=pl.CostEstimate(flops=8 * rows * width, bytes_accessed=4 * rows * width, transcendentals=rows),
    )(x, gain, order)


def context_kernel(modes, u_ref, mask_ref, rates_ref, behind_ref, out_ref):
    rows, chans = u_ref.shape
    behind = behind_ref[0]
    lane = 128
    back = (7 - lax.broadcasted_iota(jnp.int32, (8, lane), 0)).astype(F32)
    back = back + behind.astype(F32)
    for at in range(0, chans, lane):
        rates = [rates_ref[m : m + 1, at : at + lane] for m in range(modes)]
        decays = [jnp.broadcast_to(jnp.exp(-8.0 * r), (8, lane)) for r in rates]
        sums = [jnp.zeros((8, lane), F32)] * modes
        for group in range(0, rows, 16):
            value = u_ref[group : group + 16, at : at + lane].astype(F32)
            value = jnp.where(mask_ref[group : group + 16, :] != 0, value, 0.0)
            for part in (value[:8], value[8:]):
                sums = [s * d + part for s, d in zip(sums, decays)]
        for m in range(modes):
            weight = jnp.exp(-rates[m] * back)
            out_ref[m : m + 1, at : at + lane] = jnp.sum(sums[m] * weight, axis=0, keepdims=True)


def context_sums(u, mask, rates, behind):
    rows, chans = u.shape
    modes = rates.shape[0]
    tile = min(chans, 512)
    return pl.pallas_call(
        functools.partial(context_kernel, modes),
        grid=(chans // tile,),
        out_shape=jax.ShapeDtypeStruct((modes, chans), F32),
        in_specs=[
            pl.BlockSpec((rows, tile), lambda i: (0, i)),
            pl.BlockSpec((rows, 128), lambda i: (0, 0)),
            pl.BlockSpec((modes, tile), lambda i: (0, i)),
            pl.BlockSpec(memory_space=pltpu.SMEM),
        ],
        out_specs=pl.BlockSpec((modes, tile), lambda i: (0, i)),
        compiler_params=pltpu.CompilerParams(vmem_limit_bytes=16 << 20),
        cost_estimate=pl.CostEstimate(flops=2 * rows * chans * modes, bytes_accessed=2 * rows * chans, transcendentals=8 * chans * modes),
    )(u, mask, rates, behind)


def finish_kernel(
    taps_count, half_ref, mine_ref, other_ref, tail_ref, taps_ref, rates_ref, res_ref, skip_ref, partial_ref,
    out_ref, ext, inner, spread,
):
    half_rows = mine_ref.shape[0]
    window = 2 * half_rows
    chans = out_ref.shape[1]
    modes = rates_ref.shape[0]
    place = pl.multiple_of(HALO + half_ref[0] * half_rows, 8)
    away = pl.multiple_of(HALO + (1 - half_ref[0]) * half_rows, 8)
    ext[0:HALO, :] = tail_ref[...]
    ext[pl.ds(place, half_rows), :] = mine_ref[...].astype(F32)
    ext[pl.ds(away, half_rows), :] = other_ref[...].astype(F32)

    rates = rates_ref[...]
    res = res_ref[...]
    decay8 = jnp.exp(-8.0 * rates)
    state = jnp.sum(partial_ref[...].astype(F32), axis=0)
    steps = [jnp.exp(-float(k) * rates) for k in range(8)]
    reads = [res * jnp.exp(-float(k + 1) * rates) for k in range(8)]
    direct = [jnp.sum(res * s, axis=0, keepdims=True) for s in steps]
    skip = skip_ref[...]

    chunk = 64
    inner[0:8, :] = jnp.zeros((8, chans), F32)
    for t in range(0, window, chunk):
        def conv(stream):
            lanes = slice(stream * chans, (stream + 1) * chans)
            total = jnp.zeros((chunk, chans), F32)
            for j in range(taps_count):
                row = HALO + t - j
                total = total + taps_ref[j : j + 1, lanes] * ext[row : row + chunk, lanes]
            return total

        inner[8 + t : 8 + t + chunk, :] = conv(1) * conv(2)
        for g in range(t, t + chunk, 8):
            fresh = state * decay8
            for k in range(8):
                folded = reads[k] * state
                spread[k, :, :] = folded[0:8] + folded[8:16]
                fresh = fresh + steps[7 - k] * inner[8 + g + k : 9 + g + k, :]
            far = jnp.sum(spread[...], axis=1)
            rows = lax.broadcasted_iota(jnp.int32, (8, chans), 0)
            near = (direct[0] + skip) * inner[8 + g : 16 + g, :]
            for k in range(1, 8):
                shifted = inner[8 + g - k : 16 + g - k, :]
                near = near + direct[k] * jnp.where(rows >= k, shifted, 0.0)
            state = fresh
            inner_out = far + near
            spread_out = inner_out
            ext[g : g + 8, 2 * chans :] = spread_out
        mixed = conv(0) * ext[t : t + chunk, 2 * chans :]
        out_ref[t : t + chunk, :] = mixed.astype(out_ref.dtype)


def finish(half, mine, other, tail, taps, rates, res, skip, partial):
    window = 2 * mine.shape[0]
    chans = mine.shape[1] // 3
    vmem = pl.BlockSpec(memory_space=pltpu.VMEM)
    return pl.pallas_call(
        functools.partial(finish_kernel, taps.shape[0]),
        out_shape=jax.ShapeDtypeStruct((window, chans), BF16),
        in_specs=[pl.BlockSpec(memory_space=pltpu.SMEM)] + [vmem] * 8,
        out_specs=vmem,
        scratch_shapes=[
            pltpu.VMEM((HALO + window, 3 * chans), F32),
            pltpu.VMEM((8 + window, chans), F32),
            pltpu.VMEM((8, 8, chans), F32),
        ],
        compiler_params=pltpu.CompilerParams(vmem_limit_bytes=24 << 20),
        cost_estimate=pl.CostEstimate(flops=60 * window * 3 * chans, bytes_accessed=8 * window * chans, transcendentals=0),
    )(half, mine, other, tail, taps, rates, res, skip, partial)


def ring_gather(block, axis, size):
    before = step(axis, size, 1)(block)
    after = step(axis, size, -1)(block)
    half = block.shape[0] // 2
    low = step(axis, size, 1)(before[:half])
    high = step(axis, size, -1)(after[half:])
    return block, before, after, low, high


def local(
    window_x, norm_gain, proj_weight, proj_tail, short_taps, decay_rates, residues, skip_bias, context_u, context_tokens
):
    y, xl, core = lax.axis_index("y"), lax.axis_index("xl"), lax.axis_index("core")
    xh, z = lax.axis_index("xh"), lax.axis_index("z")
    y_count, z_count = lax.axis_size("y"), lax.axis_size("z")
    seq_index = xh * z_count + z
    seq_count = 2 * z_count
    rows, width = window_x.shape[1:]
    depth, _, chans = proj_weight.shape
    cols = 3 * chans
    ctx_rows = context_u.shape[1]
    modes = decay_rates.shape[1]
    cross = step("core", 2, 1)

    spots = [((y + dy) % y_count) * 2 + (xl + fl) % 2 for dy in (0, y_count - 1, 1, 2) for fl in (0, 1)]
    order = jnp.stack([s * 2 + core for s in spots] + [s * 2 + 1 - core for s in spots]).astype(jnp.int32)
    keep, give = norm(window_x[0], norm_gain[None, :], order)
    took = cross(give)
    sent_rows = jnp.concatenate([keep, took], axis=0)
    all_rows = lax.all_gather(sent_rows, "z", axis=0, tiled=False)

    weight = proj_weight.reshape(depth, cols)
    near = jnp.concatenate([weight, step("xl", 2, 1)(weight)], axis=0)
    far = step("xh", 2, 1)(near)

    def panel(block):
        own, before, after, low, high = ring_gather(block, "y", y_count)
        return jnp.concatenate([own, before, after, low, high], axis=0)

    panel_near = panel(near)
    panel_far = panel(far)

    rates_t = decay_rates.T
    mask = jnp.broadcast_to(context_tokens[0][:, None], (ctx_rows, 128))
    behind = ((seq_count - 1 - seq_index) * ctx_rows)[None].astype(jnp.int32)
    sums = context_sums(context_u[0], mask, rates_t, behind)
    sums = sums.reshape(modes, seq_count, chans).transpose(1, 0, 2)
    partial = lax.all_to_all(sums, ("xh", "z"), split_axis=0, concat_axis=0, tiled=True)

    all_rows = all_rows.reshape(z_count, 2, rows, width // 2)
    theirs = all_rows[:, 1].reshape(z_count * rows, width // 2)
    ours = all_rows[:, 0].reshape(z_count * rows, width // 2)

    def dot(a, b):
        return jnp.dot(a, b, preferred_element_type=F32)

    got_far = cross(dot(theirs, panel_far))
    got_near = cross(dot(theirs, panel_near))
    features_far = (dot(ours, panel_far) + got_far).astype(BF16)
    other = step("xh", 2, 1)(features_far)
    mine = (dot(ours, panel_near) + got_near).astype(BF16)

    rates_local = lax.dynamic_slice_in_dim(rates_t, seq_index * chans, chans, 1)
    tail = proj_tail[0].reshape(-1, cols).astype(F32)
    tail = jnp.pad(tail, ((HALO - tail.shape[0], 0), (0, 0)))
    taps = short_taps.reshape(-1, cols)
    out = finish(xh[None].astype(jnp.int32), mine, other, tail, taps, rates_local, residues.T, skip_bias[None, :], partial)
    return out[None]


def solution(mesh):
    shape = mesh.devices.shape
    grid = Mesh(mesh.devices.reshape(shape[0] // 4, 2, 2, 2, shape[1] // 2), ("y", "xl", "core", "xh", "z"))
    design, seq = ("y", "xl", "core"), ("xh", "z")
    in_specs = (
        P(design, seq, None),
        P(),
        P(design, None, seq),
        P(design, None, None, seq),
        P(None, None, seq),
        P(),
        P(seq, None),
        P(seq),
        P(design, seq, None),
        P(design, seq),
    )
    return jax.shard_map(local, mesh=grid, in_specs=in_specs, out_specs=P(design, None, seq), check_vma=False)
```

```python
import functools

import jax
import jax.numpy as jnp
from jax import lax
from jax.experimental import pallas as pl
from jax.experimental.pallas import tpu as pltpu
from jax.sharding import Mesh
from jax.sharding import PartitionSpec as P

F32 = jnp.float32
BF16 = jnp.bfloat16
HALO = 8


def step(axis, size, by):
    return functools.partial(
        lax.ppermute, axis_name=axis, perm=[(i, (i + by) % size) for i in range(size)]
    )


def norm_kernel(blocks, x_ref, gain_ref, order_ref, out_ref):
    rows, width = x_ref.shape
    depth = width // blocks
    total = jnp.zeros((rows, depth), F32)
    for b in range(blocks):
        part = x_ref[:, b * depth : (b + 1) * depth].astype(F32)
        total = total + part * part
    scale = lax.rsqrt(jnp.sum(total, axis=1, keepdims=True) / width + 1e-6)
    for b in range(blocks):
        source = pl.multiple_of(order_ref[b] * depth, depth)
        part = x_ref[:, pl.ds(source, depth)].astype(F32)
        value = part * scale * gain_ref[:, pl.ds(source, depth)]
        out_ref[:, b * depth : (b + 1) * depth] = value.astype(BF16)


def norm(x, gain, order):
    rows, width = x.shape
    vmem = pl.BlockSpec(memory_space=pltpu.VMEM)
    return pl.pallas_call(
        functools.partial(norm_kernel, order.shape[0]),
        out_shape=jax.ShapeDtypeStruct((rows, width), BF16),
        in_specs=[vmem, vmem, pl.BlockSpec(memory_space=pltpu.SMEM)],
        out_specs=vmem,
        compiler_params=pltpu.CompilerParams(vmem_limit_bytes=16 << 20),
        cost_estimate=pl.CostEstimate(flops=8 * rows * width, bytes_accessed=4 * rows * width, transcendentals=rows),
    )(x, gain, order)


def context_kernel(modes, where_ref, u_ref, tokens_ref, rates_ref, out_ref):
    rows, chans = u_ref.shape
    lane = out_ref.shape[2]
    back = (7 - lax.broadcasted_iota(jnp.int32, (8, lane), 0)).astype(F32)
    back = back + where_ref[1].astype(F32)
    kept = (tokens_ref[...] != 0).astype(F32)
    kept = jnp.broadcast_to(kept, (rows, rows)).T[:, :lane]
    for at in range(0, chans, lane):
        rates = [rates_ref[m : m + 1, at : at + lane] for m in range(modes)]
        decays = [jnp.broadcast_to(jnp.exp(-8.0 * r), (8, lane)) for r in rates]
        sums = [jnp.zeros((8, lane), F32)] * modes
        for group in range(0, rows, 16):
            value = u_ref[group : group + 16, at : at + lane].astype(F32)
            value = jnp.where(kept[group : group + 16, :] > 0.5, value, 0.0)
            for part in (value[:8], value[8:]):
                sums = [s * d + part for s, d in zip(sums, decays)]
        for m in range(modes):
            weight = jnp.exp(-rates[m] * back)
            out_ref[at // lane, m : m + 1, :] = jnp.sum(sums[m] * weight, axis=0, keepdims=True)


def context_sums(u, tokens, rates, where, lane):
    rows, chans = u.shape
    modes = rates.shape[0]
    blocks = chans // lane
    each = min(4, blocks // 2)
    tiles = blocks // each
    tile = each * lane
    spec = pltpu.PrefetchScalarGridSpec(
        num_scalar_prefetch=1,
        grid=(tiles,),
        in_specs=[
            pl.BlockSpec((rows, tile), lambda i, w: (0, i)),
            pl.BlockSpec((1, rows), lambda i, w: (0, 0)),
            pl.BlockSpec((modes, tile), lambda i, w: (0, i)),
        ],
        out_specs=pl.BlockSpec((each, modes, lane), lambda i, w: ((i + w[0] * (tiles // 2)) % tiles, 0, 0)),
    )
    return pl.pallas_call(
        functools.partial(context_kernel, modes),
        grid_spec=spec,
        out_shape=jax.ShapeDtypeStruct((blocks, modes, lane), F32),
        compiler_params=pltpu.CompilerParams(vmem_limit_bytes=16 << 20),
        cost_estimate=pl.CostEstimate(flops=2 * rows * chans * modes, bytes_accessed=2 * rows * chans, transcendentals=8 * chans * modes),
    )(where, u, tokens, rates)


def finish_kernel(
    taps_count, half_ref, mine_ref, other_ref, tail_ref, taps_ref, rates_ref, res_ref, skip_ref, partial_ref,
    out_ref, ext, inner, spread,
):
    half_rows = mine_ref.shape[0]
    window = 2 * half_rows
    chans = out_ref.shape[1]
    modes = rates_ref.shape[0]
    place = pl.multiple_of(HALO + half_ref[0] * half_rows, 8)
    away = pl.multiple_of(HALO + (1 - half_ref[0]) * half_rows, 8)
    ext[0:HALO, :] = tail_ref[...]
    ext[pl.ds(place, half_rows), :] = mine_ref[...].astype(F32)
    ext[pl.ds(away, half_rows), :] = other_ref[...].astype(F32)

    rates = rates_ref[...]
    res = res_ref[...]
    decay8 = jnp.exp(-8.0 * rates)
    state = jnp.sum(partial_ref[...].astype(F32), axis=0)
    steps = [jnp.exp(-float(k) * rates) for k in range(8)]
    reads = [res * jnp.exp(-float(k + 1) * rates) for k in range(8)]
    direct = [jnp.sum(res * s, axis=0, keepdims=True) for s in steps]
    skip = skip_ref[...]

    chunk = 64
    inner[0:8, :] = jnp.zeros((8, chans), F32)
    for t in range(0, window, chunk):
        def conv(stream):
            lanes = slice(stream * chans, (stream + 1) * chans)
            total = jnp.zeros((chunk, chans), F32)
            for j in range(taps_count):
                row = HALO + t - j
                total = total + taps_ref[j : j + 1, lanes] * ext[row : row + chunk, lanes]
            return total

        inner[8 + t : 8 + t + chunk, :] = conv(1) * conv(2)
        for g in range(t, t + chunk, 8):
            fresh = state * decay8
            for k in range(8):
                folded = reads[k] * state
                spread[k, :, :] = folded[0:8] + folded[8:16]
                fresh = fresh + steps[7 - k] * inner[8 + g + k : 9 + g + k, :]
            far = jnp.sum(spread[...], axis=1)
            rows = lax.broadcasted_iota(jnp.int32, (8, chans), 0)
            near = (direct[0] + skip) * inner[8 + g : 16 + g, :]
            for k in range(1, 8):
                shifted = inner[8 + g - k : 16 + g - k, :]
                near = near + direct[k] * jnp.where(rows >= k, shifted, 0.0)
            state = fresh
            inner_out = far + near
            spread_out = inner_out
            ext[g : g + 8, 2 * chans :] = spread_out
        mixed = conv(0) * ext[t : t + chunk, 2 * chans :]
        out_ref[t : t + chunk, :] = mixed.astype(out_ref.dtype)


def finish(half, mine, other, tail, taps, rates, res, skip, partial):
    window = 2 * mine.shape[0]
    chans = mine.shape[1] // 3
    vmem = pl.BlockSpec(memory_space=pltpu.VMEM)
    return pl.pallas_call(
        functools.partial(finish_kernel, taps.shape[0]),
        out_shape=jax.ShapeDtypeStruct((window, chans), BF16),
        in_specs=[pl.BlockSpec(memory_space=pltpu.SMEM)] + [vmem] * 8,
        out_specs=vmem,
        scratch_shapes=[
            pltpu.VMEM((HALO + window, 3 * chans), F32),
            pltpu.VMEM((8 + window, chans), F32),
            pltpu.VMEM((8, 8, chans), F32),
        ],
        compiler_params=pltpu.CompilerParams(vmem_limit_bytes=24 << 20),
        cost_estimate=pl.CostEstimate(flops=60 * window * 3 * chans, bytes_accessed=8 * window * chans, transcendentals=0),
    )(half, mine, other, tail, taps, rates, res, skip, partial)


def ring_gather(block, axis, size):
    before = step(axis, size, 1)(block)
    after = step(axis, size, -1)(block)
    half = block.shape[0] // 2
    low = step(axis, size, 1)(before[:half])
    high = step(axis, size, -1)(after[half:])
    return block, before, after, low, high


def local(
    window_x, norm_gain, proj_weight, proj_tail, short_taps, decay_rates, residues, skip_bias, context_u, context_tokens
):
    y, xl, core = lax.axis_index("y"), lax.axis_index("xl"), lax.axis_index("core")
    xh, z = lax.axis_index("xh"), lax.axis_index("z")
    y_count, z_count = lax.axis_size("y"), lax.axis_size("z")
    seq_index = xh * z_count + z
    seq_count = 2 * z_count
    rows, width = window_x.shape[1:]
    depth, _, chans = proj_weight.shape
    cols = 3 * chans
    ctx_rows = context_u.shape[1]
    modes = decay_rates.shape[1]

    order = [
        (((y + dy) % y_count) * 2 + (xl + fl) % 2) * 2 + (xh + side) % 2
        for fl in (0, 1) for dy in (0, y_count - 1, 1, 2) for side in (0, 1)
    ]
    normed = norm(window_x[0], norm_gain[None, :], jnp.stack(order).astype(jnp.int32))
    all_rows = lax.all_gather(normed, ("z", "core"), axis=0, tiled=False)
    all_rows = all_rows.reshape(z_count, 2, rows, width)

    def swap(block, flip):
        turned = lambda c, h: (h ^ flip[0], c ^ flip[1])
        pairs = [(c * 2 + h, turned(c, h)[0] * 2 + turned(c, h)[1]) for c in (0, 1) for h in (0, 1)]
        return lax.ppermute(block, ("core", "xh"), pairs)

    weight = proj_weight.reshape(depth, cols)
    near = jnp.concatenate([swap(weight, (0, 0)), swap(weight, (0, 1))], axis=0)
    far = step("xl", 2, 1)(near)
    pieces = ring_gather(near, "y", y_count) + ring_gather(far, "y", y_count)

    rates_t = decay_rates.T
    behind = (seq_count - 1 - seq_index) * ctx_rows
    where = jnp.stack([xh, behind]).astype(jnp.int32)
    sums = context_sums(context_u[0], context_tokens, rates_t, where, chans)
    sums = sums[:z_count] + step("xh", 2, 1)(sums[z_count:])
    partial = lax.all_to_all(sums, "z", split_axis=0, concat_axis=0, tiled=True)

    panel = jnp.concatenate(pieces, axis=0)
    features = jnp.dot(all_rows.reshape(-1, width), panel, preferred_element_type=F32).astype(BF16)
    features = features.reshape(z_count, 2, rows, cols)

    def design(index):
        return lax.dynamic_index_in_dim(features, index, 1, keepdims=False).reshape(z_count * rows, cols)

    first = swap(design(xh), (0, 0))
    second = swap(design(1 - xh), (1, 0))

    rates_local = lax.dynamic_slice_in_dim(rates_t, seq_index * chans, chans, 1)
    tail = proj_tail[0].reshape(-1, cols).astype(F32)
    tail = jnp.pad(tail, ((HALO - tail.shape[0], 0), (0, 0)))
    taps = short_taps.reshape(-1, cols)
    out = finish(core[None].astype(jnp.int32), first, second, tail, taps, rates_local, residues.T, skip_bias[None, :], partial)
    return out[None]


def solution(mesh):
    shape = mesh.devices.shape
    grid = Mesh(mesh.devices.reshape(shape[0] // 4, 2, 2, 2, shape[1] // 2), ("y", "xl", "core", "xh", "z"))
    design, seq = ("y", "xl", "core"), ("xh", "z")
    in_specs = (
        P(design, seq, None),
        P(),
        P(design, None, seq),
        P(design, None, None, seq),
        P(None, None, seq),
        P(),
        P(seq, None),
        P(seq),
        P(design, seq, None),
        P(design, seq),
    )
    return jax.shard_map(local, mesh=grid, in_specs=in_specs, out_specs=P(design, None, seq), check_vma=False)
```

```python
import functools

import jax
import jax.numpy as jnp
from jax import lax
from jax.experimental import pallas as pl
from jax.experimental.pallas import tpu as pltpu
from jax.sharding import Mesh
from jax.sharding import PartitionSpec as P

F32 = jnp.float32
BF16 = jnp.bfloat16
HALO = 8


def step(axis, size, by):
    return functools.partial(
        lax.ppermute, axis_name=axis, perm=[(i, (i + by) % size) for i in range(size)]
    )


def norm_kernel(blocks, x_ref, gain_ref, order_ref, out_ref):
    rows, width = x_ref.shape
    depth = width // blocks
    total = jnp.zeros((rows, depth), F32)
    for b in range(blocks):
        part = x_ref[:, b * depth : (b + 1) * depth].astype(F32)
        total = total + part * part
    scale = lax.rsqrt(jnp.sum(total, axis=1, keepdims=True) / width + 1e-6)
    for b in range(blocks):
        source = pl.multiple_of(order_ref[b] * depth, depth)
        part = x_ref[:, pl.ds(source, depth)].astype(F32)
        value = part * scale * gain_ref[:, pl.ds(source, depth)]
        out_ref[:, b * depth : (b + 1) * depth] = value.astype(BF16)


def norm(x, gain, order):
    rows, width = x.shape
    vmem = pl.BlockSpec(memory_space=pltpu.VMEM)
    return pl.pallas_call(
        functools.partial(norm_kernel, order.shape[0]),
        out_shape=jax.ShapeDtypeStruct((rows, width), BF16),
        in_specs=[vmem, vmem, pl.BlockSpec(memory_space=pltpu.SMEM)],
        out_specs=vmem,
        compiler_params=pltpu.CompilerParams(vmem_limit_bytes=16 << 20),
        cost_estimate=pl.CostEstimate(flops=8 * rows * width, bytes_accessed=4 * rows * width, transcendentals=rows),
    )(x, gain, order)


def project_kernel(first_ref, rows_ref, *refs):
    *pieces, a_ref, b_ref, held, panel, total, row_sems, piece_sems = refs
    chunks, depth = held.shape[0], held.shape[-1]
    z_count, _, own_rows, cols = total.shape
    count = z_count * 2 * own_rows
    starts = [0]
    for piece in pieces:
        starts.append(starts[-1] + piece.shape[0])
    row_copies = [
        pltpu.make_async_copy(rows_ref.at[:, :, :, i * depth : (i + 1) * depth], held.at[i], row_sems.at[i])
        for i in range(chunks)
    ]
    piece_copies = [
        pltpu.make_async_copy(piece, panel.at[starts[p] : starts[p + 1], :], piece_sems.at[p])
        for p, piece in enumerate(pieces)
    ]
    sent = 0
    for i in range(chunks):
        while sent < len(pieces) and starts[sent] < (i + 1) * depth:
            piece_copies[sent].start()
            sent += 1
        row_copies[i].start()
    used = 0
    for i in range(chunks):
        while used < len(pieces) and starts[used] < (i + 1) * depth:
            piece_copies[used].wait()
            used += 1
        row_copies[i].wait()
        rows = held[i].reshape(count, depth)
        part = jnp.dot(rows, panel[i * depth : (i + 1) * depth, :], preferred_element_type=F32)
        part = part.reshape(total.shape)
        if i == 0:
            total[...] = part
        else:
            total[...] += part
    first = first_ref[0]
    a_ref[...] = total[:, pl.ds(first, 1)].reshape(z_count * own_rows, cols).astype(a_ref.dtype)
    b_ref[...] = total[:, pl.ds(1 - first, 1)].reshape(z_count * own_rows, cols).astype(b_ref.dtype)


def project(first, rows, pieces):
    z_count, designs, own_rows, width = rows.shape
    depth, cols = pieces[0].shape
    chunks = width // depth
    vmem = pl.BlockSpec(memory_space=pltpu.VMEM)
    shape = jax.ShapeDtypeStruct((z_count * own_rows, cols), BF16)
    return pl.pallas_call(
        project_kernel,
        out_shape=(shape, shape),
        in_specs=[pl.BlockSpec(memory_space=pltpu.SMEM)] + [pl.BlockSpec(memory_space=pltpu.HBM)] + [pl.BlockSpec(memory_space=pl.ANY)] * len(pieces),
        out_specs=(vmem, vmem),
        scratch_shapes=[
            pltpu.VMEM((chunks, z_count, designs, own_rows, depth), BF16),
            pltpu.VMEM((width, cols), BF16),
            pltpu.VMEM((z_count, designs, own_rows, cols), F32),
            pltpu.SemaphoreType.DMA((chunks,)),
            pltpu.SemaphoreType.DMA((len(pieces),)),
        ],
        compiler_params=pltpu.CompilerParams(vmem_limit_bytes=56 << 20),
        cost_estimate=pl.CostEstimate(
            flops=4 * z_count * own_rows * width * cols, bytes_accessed=2 * width * (2 * z_count * own_rows + cols), transcendentals=0
        ),
    )(first, rows, *pieces)


def context_kernel(modes, where_ref, u_ref, tokens_ref, rates_ref, out_ref):
    rows, chans = u_ref.shape
    lane = out_ref.shape[2]
    back = (7 - lax.broadcasted_iota(jnp.int32, (8, lane), 0)).astype(F32)
    back = back + where_ref[1].astype(F32)
    kept = (tokens_ref[...] != 0).astype(F32)
    kept = jnp.broadcast_to(kept, (rows, rows)).T[:, :lane]
    for at in range(0, chans, lane):
        rates = [rates_ref[m : m + 1, at : at + lane] for m in range(modes)]
        decays = [jnp.broadcast_to(jnp.exp(-8.0 * r), (8, lane)) for r in rates]
        sums = [jnp.zeros((8, lane), F32)] * modes
        for group in range(0, rows, 16):
            value = u_ref[group : group + 16, at : at + lane].astype(F32)
            value = jnp.where(kept[group : group + 16, :] > 0.5, value, 0.0)
            for part in (value[:8], value[8:]):
                sums = [s * d + part for s, d in zip(sums, decays)]
        for m in range(modes):
            weight = jnp.exp(-rates[m] * back)
            out_ref[at // lane, m : m + 1, :] = jnp.sum(sums[m] * weight, axis=0, keepdims=True)


def context_sums(u, tokens, rates, where, lane):
    rows, chans = u.shape
    modes = rates.shape[0]
    blocks = chans // lane
    each = min(4, blocks // 2)
    tiles = blocks // each
    tile = each * lane
    spec = pltpu.PrefetchScalarGridSpec(
        num_scalar_prefetch=1,
        grid=(tiles,),
        in_specs=[
            pl.BlockSpec((rows, tile), lambda i, w: (0, i)),
            pl.BlockSpec((1, rows), lambda i, w: (0, 0)),
            pl.BlockSpec((modes, tile), lambda i, w: (0, i)),
        ],
        out_specs=pl.BlockSpec((each, modes, lane), lambda i, w: ((i + w[0] * (tiles // 2)) % tiles, 0, 0)),
    )
    return pl.pallas_call(
        functools.partial(context_kernel, modes),
        grid_spec=spec,
        out_shape=jax.ShapeDtypeStruct((blocks, modes, lane), F32),
        compiler_params=pltpu.CompilerParams(vmem_limit_bytes=16 << 20),
        cost_estimate=pl.CostEstimate(flops=2 * rows * chans * modes, bytes_accessed=2 * rows * chans, transcendentals=8 * chans * modes),
    )(where, u, tokens, rates)


def finish_kernel(
    taps_count, half_ref, mine_ref, other_ref, tail_ref, taps_ref, rates_ref, res_ref, skip_ref, partial_ref,
    out_ref, ext, inner, spread,
):
    half_rows = mine_ref.shape[0]
    window = 2 * half_rows
    chans = out_ref.shape[1]
    modes = rates_ref.shape[0]
    place = pl.multiple_of(HALO + half_ref[0] * half_rows, 8)
    away = pl.multiple_of(HALO + (1 - half_ref[0]) * half_rows, 8)
    ext[0:HALO, :] = tail_ref[...]
    ext[pl.ds(place, half_rows), :] = mine_ref[...].astype(F32)
    ext[pl.ds(away, half_rows), :] = other_ref[...].astype(F32)

    rates = rates_ref[...]
    res = res_ref[...]
    decay8 = jnp.exp(-8.0 * rates)
    state = jnp.sum(partial_ref[...].astype(F32), axis=0)
    steps = [jnp.exp(-float(k) * rates) for k in range(8)]
    reads = [res * jnp.exp(-float(k + 1) * rates) for k in range(8)]
    direct = [jnp.sum(res * s, axis=0, keepdims=True) for s in steps]
    skip = skip_ref[...]

    chunk = 64
    inner[0:8, :] = jnp.zeros((8, chans), F32)
    for t in range(0, window, chunk):
        def conv(stream):
            lanes = slice(stream * chans, (stream + 1) * chans)
            total = jnp.zeros((chunk, chans), F32)
            for j in range(taps_count):
                row = HALO + t - j
                total = total + taps_ref[j : j + 1, lanes] * ext[row : row + chunk, lanes]
            return total

        inner[8 + t : 8 + t + chunk, :] = conv(1) * conv(2)
        for g in range(t, t + chunk, 8):
            fresh = state * decay8
            for k in range(8):
                folded = reads[k] * state
                spread[k, :, :] = folded[0:8] + folded[8:16]
                fresh = fresh + steps[7 - k] * inner[8 + g + k : 9 + g + k, :]
            far = jnp.sum(spread[...], axis=1)
            rows = lax.broadcasted_iota(jnp.int32, (8, chans), 0)
            near = (direct[0] + skip) * inner[8 + g : 16 + g, :]
            for k in range(1, 8):
                shifted = inner[8 + g - k : 16 + g - k, :]
                near = near + direct[k] * jnp.where(rows >= k, shifted, 0.0)
            state = fresh
            inner_out = far + near
            spread_out = inner_out
            ext[g : g + 8, 2 * chans :] = spread_out
        mixed = conv(0) * ext[t : t + chunk, 2 * chans :]
        out_ref[t : t + chunk, :] = mixed.astype(out_ref.dtype)


def finish(half, mine, other, tail, taps, rates, res, skip, partial):
    window = 2 * mine.shape[0]
    chans = mine.shape[1] // 3
    vmem = pl.BlockSpec(memory_space=pltpu.VMEM)
    return pl.pallas_call(
        functools.partial(finish_kernel, taps.shape[0]),
        out_shape=jax.ShapeDtypeStruct((window, chans), BF16),
        in_specs=[pl.BlockSpec(memory_space=pltpu.SMEM)] + [vmem] * 8,
        out_specs=vmem,
        scratch_shapes=[
            pltpu.VMEM((HALO + window, 3 * chans), F32),
            pltpu.VMEM((8 + window, chans), F32),
            pltpu.VMEM((8, 8, chans), F32),
        ],
        compiler_params=pltpu.CompilerParams(vmem_limit_bytes=24 << 20),
        cost_estimate=pl.CostEstimate(flops=60 * window * 3 * chans, bytes_accessed=8 * window * chans, transcendentals=0),
    )(half, mine, other, tail, taps, rates, res, skip, partial)


def ring_ends(before, after, axis, size):
    half = before.shape[0] // 2
    return step(axis, size, 1)(before[:half]), step(axis, size, -1)(after[half:])


def ring_gather(block, axis, size):
    before = step(axis, size, 1)(block)
    after = step(axis, size, -1)(block)
    return (block, before, after) + ring_ends(before, after, axis, size)


def local(
    window_x, norm_gain, proj_weight, proj_tail, short_taps, decay_rates, residues, skip_bias, context_u, context_tokens
):
    y, xl, core = lax.axis_index("y"), lax.axis_index("xl"), lax.axis_index("core")
    xh, z = lax.axis_index("xh"), lax.axis_index("z")
    y_count, z_count = lax.axis_size("y"), lax.axis_size("z")
    seq_index = xh * z_count + z
    seq_count = 2 * z_count
    rows, width = window_x.shape[1:]
    depth, _, chans = proj_weight.shape
    cols = 3 * chans
    ctx_rows = context_u.shape[1]
    modes = decay_rates.shape[1]

    order = [
        (((y + dy) % y_count) * 2 + (xl + fl) % 2) * 2 + (xh + side) % 2
        for fl in (0, 1) for dy in (0, y_count - 1, 1, 2) for side in (0, 1)
    ]
    normed = norm(window_x[0], norm_gain[None, :], jnp.stack(order).astype(jnp.int32))
    all_rows = lax.all_gather(normed, ("z", "core"), axis=0, tiled=False)
    all_rows = all_rows.reshape(z_count, 2, rows, width)

    def swap(block, flip):
        turned = lambda c, h: (h ^ flip[0], c ^ flip[1])
        pairs = [(c * 2 + h, turned(c, h)[0] * 2 + turned(c, h)[1]) for c in (0, 1) for h in (0, 1)]
        return lax.ppermute(block, ("core", "xh"), pairs)

    weight = proj_weight.reshape(depth, cols)
    near = jnp.concatenate([swap(weight, (0, 0)), swap(weight, (0, 1))], axis=0)
    far = step("xl", 2, 1)(near)

    rates_t = decay_rates.T
    behind = (seq_count - 1 - seq_index) * ctx_rows
    where = jnp.stack([xh, behind]).astype(jnp.int32)
    sums = context_sums(context_u[0], context_tokens, rates_t, where, chans)
    far, sums = lax.optimization_barrier((far, sums))
    near_pieces = ring_gather(near, "y", y_count)
    sums = sums[:z_count] + step("xh", 2, 1)(sums[z_count:])
    before, after = (step("y", y_count, by)(far) for by in (1, -1))
    before, after, sums = lax.optimization_barrier((before, after, sums))
    pieces = near_pieces + (far, before, after) + ring_ends(before, after, "y", y_count)
    partial = lax.all_to_all(sums, "z", split_axis=0, concat_axis=0, tiled=True)

    first, second = project(xh[None].astype(jnp.int32), all_rows, pieces)
    first = swap(first, (0, 0))
    second = swap(second, (1, 0))

    rates_local = lax.dynamic_slice_in_dim(rates_t, seq_index * chans, chans, 1)
    tail = proj_tail[0].reshape(-1, cols).astype(F32)
    tail = jnp.pad(tail, ((HALO - tail.shape[0], 0), (0, 0)))
    taps = short_taps.reshape(-1, cols)
    out = finish(core[None].astype(jnp.int32), first, second, tail, taps, rates_local, residues.T, skip_bias[None, :], partial)
    return out[None]


def solution(mesh):
    shape = mesh.devices.shape
    grid = Mesh(mesh.devices.reshape(shape[0] // 4, 2, 2, 2, shape[1] // 2), ("y", "xl", "core", "xh", "z"))
    design, seq = ("y", "xl", "core"), ("xh", "z")
    in_specs = (
        P(design, seq, None),
        P(),
        P(design, None, seq),
        P(design, None, None, seq),
        P(None, None, seq),
        P(),
        P(seq, None),
        P(seq),
        P(design, seq, None),
        P(design, seq),
    )
    return jax.shard_map(local, mesh=grid, in_specs=in_specs, out_specs=P(design, None, seq), check_vma=False)
```

```python
import functools

import jax
import jax.numpy as jnp
from jax import lax
from jax.experimental import pallas as pl
from jax.experimental.pallas import tpu as pltpu
from jax.sharding import Mesh
from jax.sharding import PartitionSpec as P

F32 = jnp.float32
BF16 = jnp.bfloat16
HALO = 8


def step(axis, size, by):
    return functools.partial(
        lax.ppermute, axis_name=axis, perm=[(i, (i + by) % size) for i in range(size)]
    )


def norm_kernel(blocks, x_ref, gain_ref, order_ref, out_ref):
    rows, width = x_ref.shape
    depth = width // blocks
    total = jnp.zeros((rows, depth), F32)
    for b in range(blocks):
        part = x_ref[:, b * depth : (b + 1) * depth].astype(F32)
        total = total + part * part
    scale = lax.rsqrt(jnp.sum(total, axis=1, keepdims=True) / width + 1e-6)
    for b in range(blocks):
        source = pl.multiple_of(order_ref[b] * depth, depth)
        part = x_ref[:, pl.ds(source, depth)].astype(F32)
        value = part * scale * gain_ref[:, pl.ds(source, depth)]
        out_ref[:, b * depth : (b + 1) * depth] = value.astype(BF16)


def norm(x, gain, order):
    rows, width = x.shape
    vmem = pl.BlockSpec(memory_space=pltpu.VMEM)
    return pl.pallas_call(
        functools.partial(norm_kernel, order.shape[0]),
        out_shape=jax.ShapeDtypeStruct((rows, width), BF16),
        in_specs=[vmem, vmem, pl.BlockSpec(memory_space=pltpu.SMEM)],
        out_specs=vmem,
        compiler_params=pltpu.CompilerParams(vmem_limit_bytes=16 << 20),
        cost_estimate=pl.CostEstimate(flops=8 * rows * width, bytes_accessed=4 * rows * width, transcendentals=rows),
    )(x, gain, order)


def project_kernel(first_ref, rows_ref, *refs):
    *pieces, a_ref, b_ref, held, panel, total, row_sems, piece_sems = refs
    chunks, depth = held.shape[0], held.shape[-1]
    z_count, _, own_rows, cols = total.shape
    count = z_count * 2 * own_rows
    starts = [0]
    for piece in pieces:
        starts.append(starts[-1] + piece.shape[0])
    row_copies = [
        pltpu.make_async_copy(rows_ref.at[:, :, :, i * depth : (i + 1) * depth], held.at[i], row_sems.at[i])
        for i in range(chunks)
    ]
    piece_copies = [
        pltpu.make_async_copy(piece, panel.at[starts[p] : starts[p + 1], :], piece_sems.at[p])
        for p, piece in enumerate(pieces)
    ]
    sent = 0
    for i in range(chunks):
        while sent < len(pieces) and starts[sent] < (i + 1) * depth:
            piece_copies[sent].start()
            sent += 1
        row_copies[i].start()
    used = 0
    for i in range(chunks):
        while used < len(pieces) and starts[used] < (i + 1) * depth:
            piece_copies[used].wait()
            used += 1
        row_copies[i].wait()
        rows = held[i].reshape(count, depth)
        part = jnp.dot(rows, panel[i * depth : (i + 1) * depth, :], preferred_element_type=F32)
        part = part.reshape(total.shape)
        if i == 0:
            total[...] = part
        else:
            total[...] += part
    first = first_ref[0]
    a_ref[...] = total[:, pl.ds(first, 1)].reshape(z_count * own_rows, cols).astype(a_ref.dtype)
    b_ref[...] = total[:, pl.ds(1 - first, 1)].reshape(z_count * own_rows, cols).astype(b_ref.dtype)


def project(first, rows, pieces):
    z_count, designs, own_rows, width = rows.shape
    depth, cols = pieces[0].shape
    chunks = width // depth
    vmem = pl.BlockSpec(memory_space=pltpu.VMEM)
    shape = jax.ShapeDtypeStruct((z_count * own_rows, cols), BF16)
    return pl.pallas_call(
        project_kernel,
        out_shape=(shape, shape),
        in_specs=[pl.BlockSpec(memory_space=pltpu.SMEM)] + [pl.BlockSpec(memory_space=pltpu.HBM)] + [pl.BlockSpec(memory_space=pl.ANY)] * len(pieces),
        out_specs=(vmem, vmem),
        scratch_shapes=[
            pltpu.VMEM((chunks, z_count, designs, own_rows, depth), BF16),
            pltpu.VMEM((width, cols), BF16),
            pltpu.VMEM((z_count, designs, own_rows, cols), F32),
            pltpu.SemaphoreType.DMA((chunks,)),
            pltpu.SemaphoreType.DMA((len(pieces),)),
        ],
        compiler_params=pltpu.CompilerParams(vmem_limit_bytes=56 << 20),
        cost_estimate=pl.CostEstimate(
            flops=4 * z_count * own_rows * width * cols, bytes_accessed=2 * width * (2 * z_count * own_rows + cols), transcendentals=0
        ),
    )(first, rows, *pieces)


def context_kernel(modes, where_ref, u_ref, tokens_ref, rates_ref, out_ref):
    rows, chans = u_ref.shape
    lane = out_ref.shape[2]
    back = (7 - lax.broadcasted_iota(jnp.int32, (8, lane), 0)).astype(F32)
    back = back + where_ref[1].astype(F32)
    kept = (tokens_ref[...] != 0).astype(F32)
    kept = jnp.broadcast_to(kept, (rows, rows)).T[:, :lane]
    for at in range(0, chans, lane):
        rates = [rates_ref[m : m + 1, at : at + lane] for m in range(modes)]
        decays = [jnp.broadcast_to(jnp.exp(-8.0 * r), (8, lane)) for r in rates]
        sums = [jnp.zeros((8, lane), F32)] * modes
        for group in range(0, rows, 16):
            value = u_ref[group : group + 16, at : at + lane].astype(F32)
            value = jnp.where(kept[group : group + 16, :] > 0.5, value, 0.0)
            for part in (value[:8], value[8:]):
                sums = [s * d + part for s, d in zip(sums, decays)]
        for m in range(modes):
            weight = jnp.exp(-rates[m] * back)
            out_ref[at // lane, m : m + 1, :] = jnp.sum(sums[m] * weight, axis=0, keepdims=True)


def context_sums(u, tokens, rates, where, lane):
    rows, chans = u.shape
    modes = rates.shape[0]
    blocks = chans // lane
    each = min(4, blocks // 2)
    tiles = blocks // each
    tile = each * lane
    spec = pltpu.PrefetchScalarGridSpec(
        num_scalar_prefetch=1,
        grid=(tiles,),
        in_specs=[
            pl.BlockSpec((rows, tile), lambda i, w: (0, i)),
            pl.BlockSpec((1, rows), lambda i, w: (0, 0)),
            pl.BlockSpec((modes, tile), lambda i, w: (0, i)),
        ],
        out_specs=pl.BlockSpec((each, modes, lane), lambda i, w: ((i + w[0] * (tiles // 2)) % tiles, 0, 0)),
    )
    return pl.pallas_call(
        functools.partial(context_kernel, modes),
        grid_spec=spec,
        out_shape=jax.ShapeDtypeStruct((blocks, modes, lane), F32),
        compiler_params=pltpu.CompilerParams(vmem_limit_bytes=16 << 20),
        cost_estimate=pl.CostEstimate(flops=2 * rows * chans * modes, bytes_accessed=2 * rows * chans, transcendentals=8 * chans * modes),
    )(where, u, tokens, rates)


def finish_kernel(
    taps_count, half_ref, mine_ref, other_ref, tail_ref, taps_ref, rates_ref, res_ref, skip_ref, partial_ref,
    out_ref, ext, inner, spread,
):
    half_rows = mine_ref.shape[0]
    window = 2 * half_rows
    chans = out_ref.shape[1]
    modes = rates_ref.shape[0]
    place = pl.multiple_of(HALO + half_ref[0] * half_rows, 8)
    away = pl.multiple_of(HALO + (1 - half_ref[0]) * half_rows, 8)
    ext[0:HALO, :] = tail_ref[...]
    ext[pl.ds(place, half_rows), :] = mine_ref[...].astype(F32)
    ext[pl.ds(away, half_rows), :] = other_ref[...].astype(F32)

    rates = rates_ref[...]
    res = res_ref[...]
    decay8 = jnp.exp(-8.0 * rates)
    state = jnp.sum(partial_ref[...].astype(F32), axis=0)
    steps = [jnp.exp(-float(k) * rates) for k in range(8)]
    reads = [res * jnp.exp(-float(k + 1) * rates) for k in range(8)]
    direct = [jnp.sum(res * s, axis=0, keepdims=True) for s in steps]
    skip = skip_ref[...]

    chunk = 64
    inner[0:8, :] = jnp.zeros((8, chans), F32)
    for t in range(0, window, chunk):
        def conv(stream):
            lanes = slice(stream * chans, (stream + 1) * chans)
            total = jnp.zeros((chunk, chans), F32)
            for j in range(taps_count):
                row = HALO + t - j
                total = total + taps_ref[j : j + 1, lanes] * ext[row : row + chunk, lanes]
            return total

        inner[8 + t : 8 + t + chunk, :] = conv(1) * conv(2)
        for g in range(t, t + chunk, 8):
            fresh = state * decay8
            for k in range(8):
                folded = reads[k] * state
                spread[k, :, :] = folded[0:8] + folded[8:16]
                fresh = fresh + steps[7 - k] * inner[8 + g + k : 9 + g + k, :]
            far = jnp.sum(spread[...], axis=1)
            rows = lax.broadcasted_iota(jnp.int32, (8, chans), 0)
            near = (direct[0] + skip) * inner[8 + g : 16 + g, :]
            for k in range(1, 8):
                shifted = inner[8 + g - k : 16 + g - k, :]
                near = near + direct[k] * jnp.where(rows >= k, shifted, 0.0)
            state = fresh
            inner_out = far + near
            spread_out = inner_out
            ext[g : g + 8, 2 * chans :] = spread_out
        mixed = conv(0) * ext[t : t + chunk, 2 * chans :]
        out_ref[t : t + chunk, :] = mixed.astype(out_ref.dtype)


def finish(half, mine, other, tail, taps, rates, res, skip, partial):
    window = 2 * mine.shape[0]
    chans = mine.shape[1] // 3
    vmem = pl.BlockSpec(memory_space=pltpu.VMEM)
    return pl.pallas_call(
        functools.partial(finish_kernel, taps.shape[0]),
        out_shape=jax.ShapeDtypeStruct((window, chans), BF16),
        in_specs=[pl.BlockSpec(memory_space=pltpu.SMEM)] + [vmem] * 8,
        out_specs=vmem,
        scratch_shapes=[
            pltpu.VMEM((HALO + window, 3 * chans), F32),
            pltpu.VMEM((8 + window, chans), F32),
            pltpu.VMEM((8, 8, chans), F32),
        ],
        compiler_params=pltpu.CompilerParams(vmem_limit_bytes=24 << 20),
        cost_estimate=pl.CostEstimate(flops=60 * window * 3 * chans, bytes_accessed=8 * window * chans, transcendentals=0),
    )(half, mine, other, tail, taps, rates, res, skip, partial)


def ring_ends(before, after, axis, size):
    half = before.shape[0] // 2
    return step(axis, size, 1)(before[:half]), step(axis, size, -1)(after[half:])


def ring_gather(block, axis, size):
    before = step(axis, size, 1)(block)
    after = step(axis, size, -1)(block)
    return (block, before, after) + ring_ends(before, after, axis, size)


def local(
    window_x, norm_gain, proj_weight, proj_tail, short_taps, decay_rates, residues, skip_bias, context_u, context_tokens
):
    y, xl, core = lax.axis_index("y"), lax.axis_index("xl"), lax.axis_index("core")
    xh, z = lax.axis_index("xh"), lax.axis_index("z")
    y_count, z_count = lax.axis_size("y"), lax.axis_size("z")
    seq_index = xh * z_count + z
    seq_count = 2 * z_count
    rows, width = window_x.shape[1:]
    depth, _, chans = proj_weight.shape
    cols = 3 * chans
    ctx_rows = context_u.shape[1]
    modes = decay_rates.shape[1]

    order = [
        (((y + dy) % y_count) * 2 + (xl + fl) % 2) * 2 + (xh + side) % 2
        for fl in (0, 1) for dy in (0, y_count - 1, 1, 2) for side in (0, 1)
    ]
    normed = norm(window_x[0], norm_gain[None, :], jnp.stack(order).astype(jnp.int32))
    all_rows = lax.all_gather(normed, ("z", "core"), axis=0, tiled=False)
    all_rows = all_rows.reshape(z_count, 2, rows, width)

    def swap(block, flip):
        turned = lambda c, h: (h ^ flip[0], c ^ flip[1])
        pairs = [(c * 2 + h, turned(c, h)[0] * 2 + turned(c, h)[1]) for c in (0, 1) for h in (0, 1)]
        return lax.ppermute(block, ("core", "xh"), pairs)

    weight = proj_weight.reshape(depth, cols)
    near = jnp.concatenate([swap(weight, (0, 0)), swap(weight, (0, 1))], axis=0)
    far = step("xl", 2, 1)(near)

    rates_t = decay_rates.T
    behind = (seq_count - 1 - seq_index) * ctx_rows
    where = jnp.stack([xh, behind]).astype(jnp.int32)
    sums = context_sums(context_u[0], context_tokens, rates_t, where, chans)
    far, sums = lax.optimization_barrier((far, sums))
    near_pieces = ring_gather(near, "y", y_count)
    sums = sums[:z_count] + step("xh", 2, 1)(sums[z_count:])
    before, after = (step("y", y_count, by)(far) for by in (1, -1))
    *near_pieces, low, high, sums = lax.optimization_barrier((*near_pieces, sums))
    far_ends = (step("xl", 2, 1)(low), step("xl", 2, 1)(high))
    pieces = (*near_pieces, low, high, far, before, after, *far_ends)
    partial = lax.all_to_all(sums, "z", split_axis=0, concat_axis=0, tiled=True)

    first, second = project(xh[None].astype(jnp.int32), all_rows, pieces)
    first = swap(first, (0, 0))
    second = swap(second, (1, 0))

    rates_local = lax.dynamic_slice_in_dim(rates_t, seq_index * chans, chans, 1)
    tail = proj_tail[0].reshape(-1, cols).astype(F32)
    tail = jnp.pad(tail, ((HALO - tail.shape[0], 0), (0, 0)))
    taps = short_taps.reshape(-1, cols)
    out = finish(core[None].astype(jnp.int32), first, second, tail, taps, rates_local, residues.T, skip_bias[None, :], partial)
    return out[None]


def solution(mesh):
    shape = mesh.devices.shape
    grid = Mesh(mesh.devices.reshape(shape[0] // 4, 2, 2, 2, shape[1] // 2), ("y", "xl", "core", "xh", "z"))
    design, seq = ("y", "xl", "core"), ("xh", "z")
    in_specs = (
        P(design, seq, None),
        P(),
        P(design, None, seq),
        P(design, None, None, seq),
        P(None, None, seq),
        P(),
        P(seq, None),
        P(seq),
        P(design, seq, None),
        P(design, seq),
    )
    return jax.shard_map(local, mesh=grid, in_specs=in_specs, out_specs=P(design, None, seq), check_vma=False)
```

```python
import functools

import jax
import jax.numpy as jnp
from jax import lax
from jax.experimental import pallas as pl
from jax.experimental.pallas import tpu as pltpu
from jax.sharding import Mesh
from jax.sharding import PartitionSpec as P

F32 = jnp.float32
BF16 = jnp.bfloat16
HALO = 8


def step(axis, size, by):
    return functools.partial(
        lax.ppermute, axis_name=axis, perm=[(i, (i + by) % size) for i in range(size)]
    )


def norm_kernel(blocks, x_ref, gain_ref, order_ref, out_ref):
    rows, width = x_ref.shape
    depth = width // blocks
    total = jnp.zeros((rows, depth), F32)
    for b in range(blocks):
        part = x_ref[:, b * depth : (b + 1) * depth].astype(F32)
        total = total + part * part
    scale = lax.rsqrt(jnp.sum(total, axis=1, keepdims=True) / width + 1e-6)
    for b in range(blocks):
        source = pl.multiple_of(order_ref[b] * depth, depth)
        part = x_ref[:, pl.ds(source, depth)].astype(F32)
        value = part * scale * gain_ref[:, pl.ds(source, depth)]
        out_ref[:, b * depth : (b + 1) * depth] = value.astype(BF16)


def norm(x, gain, order):
    rows, width = x.shape
    vmem = pl.BlockSpec(memory_space=pltpu.VMEM)
    return pl.pallas_call(
        functools.partial(norm_kernel, order.shape[0]),
        out_shape=jax.ShapeDtypeStruct((rows, width), BF16),
        in_specs=[vmem, vmem, pl.BlockSpec(memory_space=pltpu.SMEM)],
        out_specs=vmem,
        compiler_params=pltpu.CompilerParams(vmem_limit_bytes=16 << 20),
        cost_estimate=pl.CostEstimate(flops=8 * rows * width, bytes_accessed=4 * rows * width, transcendentals=rows),
    )(x, gain, order)


def project_kernel(first_ref, rows_ref, *refs):
    *pieces, a_ref, b_ref, held, panel, total, row_sems, piece_sems = refs
    chunks, depth = held.shape[0], held.shape[-1]
    z_count, _, own_rows, cols = total.shape
    count = z_count * 2 * own_rows
    starts = [0]
    for piece in pieces:
        starts.append(starts[-1] + piece.shape[0])
    row_copies = [
        pltpu.make_async_copy(rows_ref.at[:, :, :, i * depth : (i + 1) * depth], held.at[i], row_sems.at[i])
        for i in range(chunks)
    ]
    piece_copies = [
        pltpu.make_async_copy(piece, panel.at[starts[p] : starts[p + 1], :], piece_sems.at[p])
        for p, piece in enumerate(pieces)
    ]
    sent = 0
    for i in range(chunks):
        while sent < len(pieces) and starts[sent] < (i + 1) * depth:
            piece_copies[sent].start()
            sent += 1
        row_copies[i].start()
    used = 0
    for i in range(chunks):
        while used < len(pieces) and starts[used] < (i + 1) * depth:
            piece_copies[used].wait()
            used += 1
        row_copies[i].wait()
        rows = held[i].reshape(count, depth)
        part = jnp.dot(rows, panel[i * depth : (i + 1) * depth, :], preferred_element_type=F32)
        part = part.reshape(total.shape)
        if i == 0:
            total[...] = part
        else:
            total[...] += part
    first = first_ref[0]
    a_ref[...] = total[:, pl.ds(first, 1)].reshape(z_count * own_rows, cols).astype(a_ref.dtype)
    b_ref[...] = total[:, pl.ds(1 - first, 1)].reshape(z_count * own_rows, cols).astype(b_ref.dtype)


def project(first, rows, pieces):
    z_count, designs, own_rows, width = rows.shape
    depth, cols = pieces[0].shape
    chunks = width // depth
    vmem = pl.BlockSpec(memory_space=pltpu.VMEM)
    shape = jax.ShapeDtypeStruct((z_count * own_rows, cols), BF16)
    return pl.pallas_call(
        project_kernel,
        out_shape=(shape, shape),
        in_specs=[pl.BlockSpec(memory_space=pltpu.SMEM)] + [pl.BlockSpec(memory_space=pltpu.HBM)] + [pl.BlockSpec(memory_space=pl.ANY)] * len(pieces),
        out_specs=(vmem, vmem),
        scratch_shapes=[
            pltpu.VMEM((chunks, z_count, designs, own_rows, depth), BF16),
            pltpu.VMEM((width, cols), BF16),
            pltpu.VMEM((z_count, designs, own_rows, cols), F32),
            pltpu.SemaphoreType.DMA((chunks,)),
            pltpu.SemaphoreType.DMA((len(pieces),)),
        ],
        compiler_params=pltpu.CompilerParams(vmem_limit_bytes=56 << 20),
        cost_estimate=pl.CostEstimate(
            flops=4 * z_count * own_rows * width * cols, bytes_accessed=2 * width * (2 * z_count * own_rows + cols), transcendentals=0
        ),
    )(first, rows, *pieces)


def context_kernel(modes, where_ref, u_ref, tokens_ref, rates_ref, out_ref):
    rows, chans = u_ref.shape
    lane = out_ref.shape[2]
    back = (7 - lax.broadcasted_iota(jnp.int32, (8, lane), 0)).astype(F32)
    back = back + where_ref[1].astype(F32)
    kept = (tokens_ref[...] != 0).astype(F32)
    kept = jnp.broadcast_to(kept, (rows, rows)).T[:, :lane]
    for at in range(0, chans, lane):
        rates = [rates_ref[m : m + 1, at : at + lane] for m in range(modes)]
        decays = [jnp.broadcast_to(jnp.exp(-8.0 * r), (8, lane)) for r in rates]
        sums = [jnp.zeros((8, lane), F32)] * modes
        for group in range(0, rows, 16):
            value = u_ref[group : group + 16, at : at + lane].astype(F32)
            value = jnp.where(kept[group : group + 16, :] > 0.5, value, 0.0)
            for part in (value[:8], value[8:]):
                sums = [s * d + part for s, d in zip(sums, decays)]
        for m in range(modes):
            weight = jnp.exp(-rates[m] * back)
            out_ref[at // lane, m : m + 1, :] = jnp.sum(sums[m] * weight, axis=0, keepdims=True)


def context_sums(u, tokens, rates, where, lane):
    rows, chans = u.shape
    modes = rates.shape[0]
    blocks = chans // lane
    each = min(4, blocks // 2)
    tiles = blocks // each
    tile = each * lane
    spec = pltpu.PrefetchScalarGridSpec(
        num_scalar_prefetch=1,
        grid=(tiles,),
        in_specs=[
            pl.BlockSpec((rows, tile), lambda i, w: (0, i)),
            pl.BlockSpec((1, rows), lambda i, w: (0, 0)),
            pl.BlockSpec((modes, tile), lambda i, w: (0, i)),
        ],
        out_specs=pl.BlockSpec((each, modes, lane), lambda i, w: ((i + w[0] * (tiles // 2)) % tiles, 0, 0)),
    )
    return pl.pallas_call(
        functools.partial(context_kernel, modes),
        grid_spec=spec,
        out_shape=jax.ShapeDtypeStruct((blocks, modes, lane), F32),
        compiler_params=pltpu.CompilerParams(vmem_limit_bytes=16 << 20),
        cost_estimate=pl.CostEstimate(flops=2 * rows * chans * modes, bytes_accessed=2 * rows * chans, transcendentals=8 * chans * modes),
    )(where, u, tokens, rates)


def finish_kernel(
    taps_count, half_ref, mine_ref, other_ref, tail_ref, taps_ref, rates_ref, res_ref, skip_ref, partial_ref,
    out_ref, ext, inner, spread,
):
    half_rows = mine_ref.shape[0]
    window = 2 * half_rows
    chans = out_ref.shape[1]
    modes = rates_ref.shape[0]
    place = pl.multiple_of(HALO + half_ref[0] * half_rows, 8)
    away = pl.multiple_of(HALO + (1 - half_ref[0]) * half_rows, 8)
    ext[0:HALO, :] = tail_ref[...]
    ext[pl.ds(place, half_rows), :] = mine_ref[...].astype(F32)
    ext[pl.ds(away, half_rows), :] = other_ref[...].astype(F32)

    rates = rates_ref[...]
    res = res_ref[...]
    decay8 = jnp.exp(-8.0 * rates)
    state = jnp.sum(partial_ref[...].astype(F32), axis=0)
    steps = [jnp.exp(-float(k) * rates) for k in range(8)]
    reads = [res * jnp.exp(-float(k + 1) * rates) for k in range(8)]
    direct = [jnp.sum(res * s, axis=0, keepdims=True) for s in steps]
    skip = skip_ref[...]

    chunk = 64
    inner[0:8, :] = jnp.zeros((8, chans), F32)
    for t in range(0, window, chunk):
        def conv(stream):
            lanes = slice(stream * chans, (stream + 1) * chans)
            total = jnp.zeros((chunk, chans), F32)
            for j in range(taps_count):
                row = HALO + t - j
                total = total + taps_ref[j : j + 1, lanes] * ext[row : row + chunk, lanes]
            return total

        inner[8 + t : 8 + t + chunk, :] = conv(1) * conv(2)
        for g in range(t, t + chunk, 8):
            fresh = state * decay8
            for k in range(8):
                folded = reads[k] * state
                spread[k, :, :] = folded[0:8] + folded[8:16]
                fresh = fresh + steps[7 - k] * inner[8 + g + k : 9 + g + k, :]
            far = jnp.sum(spread[...], axis=1)
            rows = lax.broadcasted_iota(jnp.int32, (8, chans), 0)
            near = (direct[0] + skip) * inner[8 + g : 16 + g, :]
            for k in range(1, 8):
                shifted = inner[8 + g - k : 16 + g - k, :]
                near = near + direct[k] * jnp.where(rows >= k, shifted, 0.0)
            state = fresh
            inner_out = far + near
            spread_out = inner_out
            ext[g : g + 8, 2 * chans :] = spread_out
        mixed = conv(0) * ext[t : t + chunk, 2 * chans :]
        out_ref[t : t + chunk, :] = mixed.astype(out_ref.dtype)


def finish(half, mine, other, tail, taps, rates, res, skip, partial):
    window = 2 * mine.shape[0]
    chans = mine.shape[1] // 3
    vmem = pl.BlockSpec(memory_space=pltpu.VMEM)
    return pl.pallas_call(
        functools.partial(finish_kernel, taps.shape[0]),
        out_shape=jax.ShapeDtypeStruct((window, chans), BF16),
        in_specs=[pl.BlockSpec(memory_space=pltpu.SMEM)] + [vmem] * 8,
        out_specs=vmem,
        scratch_shapes=[
            pltpu.VMEM((HALO + window, 3 * chans), F32),
            pltpu.VMEM((8 + window, chans), F32),
            pltpu.VMEM((8, 8, chans), F32),
        ],
        compiler_params=pltpu.CompilerParams(vmem_limit_bytes=24 << 20),
        cost_estimate=pl.CostEstimate(flops=60 * window * 3 * chans, bytes_accessed=8 * window * chans, transcendentals=0),
    )(half, mine, other, tail, taps, rates, res, skip, partial)


def ring_ends(before, after, axis, size):
    half = before.shape[0] // 2
    return step(axis, size, 1)(before[:half]), step(axis, size, -1)(after[half:])


def ring_gather(block, axis, size):
    before = step(axis, size, 1)(block)
    after = step(axis, size, -1)(block)
    return (block, before, after) + ring_ends(before, after, axis, size)


def local(
    window_x, norm_gain, proj_weight, proj_tail, short_taps, decay_rates, residues, skip_bias, context_u, context_tokens
):
    y, xl, core = lax.axis_index("y"), lax.axis_index("xl"), lax.axis_index("core")
    xh, z = lax.axis_index("xh"), lax.axis_index("z")
    y_count, z_count = lax.axis_size("y"), lax.axis_size("z")
    seq_index = xh * z_count + z
    seq_count = 2 * z_count
    rows, width = window_x.shape[1:]
    depth, _, chans = proj_weight.shape
    cols = 3 * chans
    ctx_rows = context_u.shape[1]
    modes = decay_rates.shape[1]

    order = [
        (((y + dy) % y_count) * 2 + (xl + fl) % 2) * 2 + (xh + side) % 2
        for fl in (0, 1) for dy in (0, y_count - 1, 1, 2) for side in (0, 1)
    ]
    normed = norm(window_x[0], norm_gain[None, :], jnp.stack(order).astype(jnp.int32))
    all_rows = lax.all_gather(normed, ("z", "core"), axis=0, tiled=False)
    all_rows = all_rows.reshape(z_count, 2, rows, width)

    def swap(block, flip):
        turned = lambda c, h: (h ^ flip[0], c ^ flip[1])
        pairs = [(c * 2 + h, turned(c, h)[0] * 2 + turned(c, h)[1]) for c in (0, 1) for h in (0, 1)]
        return lax.ppermute(block, ("core", "xh"), pairs)

    weight = proj_weight.reshape(depth, cols)
    near = jnp.concatenate([swap(weight, (0, 0)), swap(weight, (0, 1))], axis=0)
    far = step("xl", 2, 1)(near)

    rates_t = decay_rates.T
    behind = (seq_count - 1 - seq_index) * ctx_rows
    where = jnp.stack([xh, behind]).astype(jnp.int32)
    sums = context_sums(context_u[0], context_tokens, rates_t, where, chans)
    near_before, near_after = (step("y", y_count, by)(near) for by in (1, -1))
    near_before, near_after, far, sums = lax.optimization_barrier((near_before, near_after, far, sums))
    near_pieces = (near, near_before, near_after) + ring_ends(near_before, near_after, "y", y_count)
    sums = sums[:z_count] + step("xh", 2, 1)(sums[z_count:])
    before, after = (step("y", y_count, by)(far) for by in (1, -1))
    *near_pieces, low, high, sums = lax.optimization_barrier((*near_pieces, sums))
    far_ends = (step("xl", 2, 1)(low), step("xl", 2, 1)(high))
    pieces = (*near_pieces, low, high, far, before, after, *far_ends)
    partial = lax.all_to_all(sums, "z", split_axis=0, concat_axis=0, tiled=True)

    first, second = project(xh[None].astype(jnp.int32), all_rows, pieces)
    first = swap(first, (0, 0))
    second = swap(second, (1, 0))

    rates_local = lax.dynamic_slice_in_dim(rates_t, seq_index * chans, chans, 1)
    tail = proj_tail[0].reshape(-1, cols).astype(F32)
    tail = jnp.pad(tail, ((HALO - tail.shape[0], 0), (0, 0)))
    taps = short_taps.reshape(-1, cols)
    out = finish(core[None].astype(jnp.int32), first, second, tail, taps, rates_local, residues.T, skip_bias[None, :], partial)
    return out[None]


def solution(mesh):
    shape = mesh.devices.shape
    grid = Mesh(mesh.devices.reshape(shape[0] // 4, 2, 2, 2, shape[1] // 2), ("y", "xl", "core", "xh", "z"))
    design, seq = ("y", "xl", "core"), ("xh", "z")
    in_specs = (
        P(design, seq, None),
        P(),
        P(design, None, seq),
        P(design, None, None, seq),
        P(None, None, seq),
        P(),
        P(seq, None),
        P(seq),
        P(design, seq, None),
        P(design, seq),
    )
    return jax.shard_map(local, mesh=grid, in_specs=in_specs, out_specs=P(design, None, seq), check_vma=False)
```
